256 devices in a mesh: group: 4 (over z_lo, core), dp: 64 (over z_hi, x, y).
Axes of the slice: x: 4, y: 4, z: 8 (z_hi: 4, z_lo: 2; z = z_hi * 2 + z_lo), core: 2. Of those that a mesh axis runs over, the one named last changes fastest.
Arguments:
- grads: bfloat16 [256, 12, 512, 512], P(('group', 'dp')), may hold values from -15000 to 15000
Outputs:
- roots: float32 [2, 12, 512, 512], P(None, None, 'dp', 'group')
The draws below stay inside these ranges and needn't reach their ends.
All inputs are finite; a program needn't handle non-finite values.
Results may differ from the reference program's by a relative error of at most 0.0003.
Values sent between devices are 32-bit elements; how exact they have to be, the bound alone decides.
No kernel may reach another device: no remote copies, remote signals or barrier semaphores. Data moves between devices by JAX's collectives and lax.ppermute only.
A program may use at most 128 MiB of HBM per device.

```python
import math
import jax
import jax.numpy as jnp
from jax import lax

BLK = 512
NB = 12
ITERS = 4
N_GROUP = 4
N_DP = 64


def draw_grads(key, part):
    base_key = jax.random.fold_in(key, 17)
    scale_key = jax.random.fold_in(base_key, 0)
    column_key = jax.random.fold_in(base_key, 1)
    device_key = jax.random.fold_in(base_key, 3)
    log_ten = math.log(10.0)
    row_top = log_ten
    row_mix = 0.6
    col_mix = 0.5
    rows_scale = jnp.exp(jax.random.uniform(scale_key, (NB, BLK), jnp.float32, 0.0, row_top))
    cols_scale = jnp.exp(jax.random.uniform(column_key, (NB, BLK), jnp.float32, 0.0, log_ten))
    rows_dev = BLK // N_DP
    positions = jnp.arange(BLK) // rows_dev

    def one_device(device):
        noise_key = jax.random.fold_in(device_key, device)
        base_noise = jnp.clip(jax.random.normal(noise_key, (NB, BLK, BLK), jnp.float32), -4.0, 4.0)
        mixed = base_noise + row_mix * jnp.roll(base_noise, 1, axis=1) + col_mix * jnp.roll(base_noise, 1, axis=2)
        boost = jnp.where(positions == device % N_DP, 3.0, 1.0).astype(jnp.float32)
        scaled = rows_scale[:, :, None] * mixed * cols_scale[:, None, :]
        scaled = scaled * boost[None, :, None] * boost[None, None, :]
        return scaled.astype(jnp.bfloat16)
    return lax.map(one_device, jnp.arange(N_GROUP * N_DP))


def setup_inputs(seed: int = 0) -> dict:
    splits = jax.random.split(jax.random.key(seed), 2)
    grads = draw_grads(jax.random.fold_in(splits[1], 71), 0)
    return dict(grads=grads)


def accumulate(running, device_grads):
    widened = device_grads.astype(jnp.float32)
    left_gram = jnp.einsum('nik,njk->nij', widened, widened, precision=lax.Precision.HIGHEST)
    right_gram = jnp.einsum('nki,nkj->nij', widened, widened, precision=lax.Precision.HIGHEST)
    return (running + jnp.stack([left_gram, right_gram]), None)

def inverse_root(matrices):
    size_n = matrices.shape[-1]
    identity = jnp.eye(size_n, dtype=jnp.float32)
    frobenius = jnp.sqrt(lax.optimization_barrier(jnp.sum(matrices * matrices, axis=(1, 2))))
    scaling = 2.5 / frobenius
    iterate = jnp.sqrt(jnp.sqrt(scaling))[:, None, None] * identity
    coupled = scaling[:, None, None] * matrices
    for sweep in range(ITERS):
        step_matrix = (5.0 * identity - coupled) * 0.25
        iterate = jnp.einsum('kij,kjl->kil', iterate, step_matrix, precision=lax.Precision.HIGHEST)
        squared = jnp.einsum('kij,kjl->kil', step_matrix, step_matrix, precision=lax.Precision.HIGHEST)
        fourth = jnp.einsum('kij,kjl->kil', squared, squared, precision=lax.Precision.HIGHEST)
        coupled = jnp.einsum('kij,kjl->kil', fourth, coupled, precision=lax.Precision.HIGHEST)
    return iterate

def reference(grads):
    start_value = jnp.zeros((2, NB, BLK, BLK), jnp.float32)
    running = lax.scan(accumulate, start_value, grads)[0]
    statistics = running * (1.0 / (N_GROUP * N_DP * BLK))
    flat_stats = statistics.reshape(2 * NB, BLK, BLK)
    return inverse_root(flat_stats).reshape(2, NB, BLK, BLK)
```

```python
import functools

import jax
import jax.numpy as jnp
from jax import lax
from jax.experimental import pallas as pl
from jax.experimental.pallas import tpu as pltpu
from jax.sharding import Mesh
from jax.sharding import PartitionSpec as P

ITERS = 4
TOP = 64
BOT = 72
UNIT = TOP + BOT
SLABS = 8
TOP_ORDERS = (("x1", "y1", "z", "x2", "y2"), ("y1", "z", "x1", "x2", "y2"), ("z", "x1", "y1", "x2", "y2"))
BOT_ORDERS = (("x2", "y2", "z", "x1", "y1"), ("y2", "z", "x2", "x1", "y1"), ("z", "x2", "y2", "x1", "y1"))
PARAMS = pltpu.CompilerParams(vmem_limit_bytes=48 * 1024 * 1024)


def place(order, flags):
    at = 0
    for name in order:
        at = at * 2 + flags[name]
    return at


def gram_kernel(part, where_ref, grads_ref, own_ref, away_ref):
    order_top, order_bot = TOP_ORDERS[part], BOT_ORDERS[part]
    step = pl.program_id(0)
    row_y, low_z, core = where_ref[1], where_ref[2], where_ref[3]
    block = grads_ref[0]
    flipped = block.T
    half = block.shape[0] // 2
    rows = lax.broadcasted_iota(jnp.int32, (half, half), 0)
    cols = lax.broadcasted_iota(jnp.int32, (half, half), 1)
    slab_rows = half // SLABS
    for side in range(2):
        lhs, rhs = (block, flipped) if side == 0 else (flipped, block)
        mult = functools.partial(jnp.dot, preferred_element_type=jnp.float32)
        corner = mult(lhs[:half], rhs[:, :half])
        cross = mult(lhs[:half], rhs[:, half:])
        last = mult(lhs[half:], rhs[:, half:])
        fold = jnp.where(rows <= cols, corner, last)
        diagonal = jnp.where(rows == cols, last, 0.0)

        def write(out_ref):
            for slab in range(SLABS):
                from_y = lax.bitwise_xor(row_y, slab // 2)
                high = lax.shift_right_logical(from_y, 1)
                flags = {
                    "x1": lax.bitwise_and(step, 1),
                    "x2": lax.shift_right_logical(step, 1),
                    "y1": lax.bitwise_xor(lax.bitwise_and(from_y, 1), high),
                    "y2": high,
                    "z": lax.bitwise_xor(low_z, slab % 2),
                }
                top = pl.multiple_of(place(order_top, flags) * TOP, 8)
                bot = pl.multiple_of(place(order_bot, flags) * BOT + 32 * TOP, 8)
                mine = slice(slab * slab_rows, (slab + 1) * slab_rows)
                out_ref[pl.ds(top, slab_rows), :] = cross[mine, :128]
                out_ref[pl.ds(top + slab_rows, slab_rows), :] = cross[mine, 128:]
                out_ref[pl.ds(bot, slab_rows), :] = fold[mine, :128]
                out_ref[pl.ds(bot + slab_rows, slab_rows), :] = fold[mine, 128:]
                side_cols = slice(0, 128) if slab < SLABS // 2 else slice(128, 256)
                line = jnp.sum(diagonal[mine, side_cols], axis=0, keepdims=True)
                out_ref[pl.ds(bot + 2 * slab_rows, 8), :] = jnp.broadcast_to(line, (8, 128))

        @pl.when(core == side)
        def _():
            write(own_ref)

        @pl.when(core != side)
        def _():
            write(away_ref)


def gram(part, where, grads):
    order = grads.shape[-1]

    def block_of(step, where_ref):
        high = lax.shift_right_logical(step, 1)
        relative = lax.bitwise_xor(lax.bitwise_and(step, 1), 3 * high)
        return (part * 4 + lax.bitwise_xor(where_ref[0], relative), 0, 0)

    shape = jax.ShapeDtypeStruct((32 * UNIT, 128), jnp.float32)
    whole = pl.BlockSpec((32 * UNIT, 128), lambda step, where_ref: (0, 0))
    return pl.pallas_call(
        functools.partial(gram_kernel, part),
        out_shape=(shape, shape),
        grid_spec=pltpu.PrefetchScalarGridSpec(
            num_scalar_prefetch=1,
            grid=(4,),
            in_specs=[pl.BlockSpec((1, order, order), block_of)],
            out_specs=(whole, whole),
        ),
        compiler_params=PARAMS,
        name=f"gram_{part}",
    )(where, grads)


def split(value):
    high = value.astype(jnp.bfloat16)
    return high, (value - high.astype(jnp.float32)).astype(jnp.bfloat16)


def product(left, right):
    mult = functools.partial(jnp.dot, preferred_element_type=jnp.float32)
    return mult(left[0], right[0]) + (mult(left[0], right[1]) + mult(left[1], right[0]))


def root_kernel(factor, where_ref, slabs_ref, out_ref, full, picked):
    half = 256
    order = 2 * half
    slab_rows = half // SLABS
    rows = lax.broadcasted_iota(jnp.int32, (half, half), 0)
    cols = lax.broadcasted_iota(jnp.int32, (half, half), 1)

    def gathered(first):
        left = jnp.concatenate([slabs_ref[s, first : first + slab_rows] for s in range(SLABS)], axis=0)
        right = jnp.concatenate(
            [slabs_ref[s, first + slab_rows : first + 2 * slab_rows] for s in range(SLABS)], axis=0
        )
        return jnp.concatenate([left, right], axis=1) * factor

    cross = gathered(0)
    fold = gathered(TOP)
    line = jnp.concatenate(
        [sum(slabs_ref[s, TOP + 64 : TOP + 65] for s in group) for group in (range(4), range(4, 8))], axis=1
    )
    turned = fold.T
    corner = jnp.where(rows <= cols, fold, turned)
    last = jnp.where(rows > cols, fold, jnp.where(rows == cols, line * factor, turned))
    matrix = jnp.concatenate(
        [jnp.concatenate([corner, cross], axis=1), jnp.concatenate([cross.T, last], axis=1)], axis=0
    )
    total = jnp.sum(jnp.sum(matrix * matrix, axis=0, keepdims=True), axis=1, keepdims=True)
    scaling = 2.5 / jnp.sqrt(total)
    coupled = scaling * matrix
    identity = (
        lax.broadcasted_iota(jnp.int32, (order, order), 0) == lax.broadcasted_iota(jnp.int32, (order, order), 1)
    ).astype(jnp.float32)
    row_y, low_z = where_ref[1], where_ref[2]
    iterate = None
    for sweep in range(ITERS):
        step_matrix = (5.0 * identity - coupled) * 0.25
        if sweep == 0:
            full[...] = jnp.sqrt(jnp.sqrt(scaling)) * step_matrix
            for chunk in range(16):
                start = pl.multiple_of(32 * chunk + 8 * row_y, 8)
                picked[8 * chunk : 8 * chunk + 8, :] = full[pl.ds(start, 8), :]
            iterate = picked[...]
        else:
            iterate = product(split(iterate), split(step_matrix))
        if sweep < ITERS - 1:
            parts = split(step_matrix)
            squared = split(product(parts, parts))
            fourth = split(product(squared, squared))
            coupled = product(fourth, split(coupled))
    for high in range(2):

        @pl.when(low_z == high)
        def _():
            for core in range(2):
                first = 128 * (2 * high + core)
                out_ref[16 * core : 16 * core + 16] = iterate[:, first : first + 128].reshape(16, 8, 128)


def inverse_root(where, slabs, factor):
    return pl.pallas_call(
        functools.partial(root_kernel, factor),
        out_shape=jax.ShapeDtypeStruct((32, 8, 128), jnp.float32),
        in_specs=[pl.BlockSpec(memory_space=pltpu.SMEM), pl.BlockSpec(memory_space=pltpu.VMEM)],
        out_specs=pl.BlockSpec(memory_space=pltpu.VMEM),
        scratch_shapes=[pltpu.VMEM((512, 512), jnp.float32), pltpu.VMEM((128, 512), jnp.float32)],
        compiler_params=PARAMS,
        name="inverse_root",
    )(where, slabs)


def swap(value, name, odd):
    if name in ("x1", "x2", "y1", "y2"):
        flip = 1 if name[1] == "1" else 3
        return lax.ppermute(value, name[0], [(i, i ^ flip) for i in range(4)])
    if not odd:
        return lax.ppermute(value, "z_lo", [(0, 1), (1, 0)])
    pairs = []
    for high in range(4):
        pairs += [(4 + high, (high + 1) % 4), ((high + 1) % 4, 4 + high)]
    return lax.ppermute(value, ("z_lo", "z_hi"), pairs)


def body(grads):
    local_grads = grads[0]
    order = local_grads.shape[1]
    where = jnp.stack([lax.axis_index(name).astype(jnp.int32) for name in ("x", "y", "z_lo", "core")])
    factor = 1.0 / (256 * order)
    lanes = []
    for part in range(3):
        own, away = gram(part, where, local_grads)
        came = lax.ppermute(away, "core", [(0, 1), (1, 0)])
        cut = 32 * TOP
        for odd, (first, size, orders) in enumerate(((0, cut, TOP_ORDERS), (cut, 32 * BOT, BOT_ORDERS))):
            middle = first + size // 2
            keep = own[first:middle] + came[first:middle]
            send = own[middle : first + size] + came[middle : first + size]
            lanes.append([orders[part], odd, keep, send])
    done = [[], []]
    for orders, odd, keep, send in lanes:
        for step in range(3):
            summed = keep + swap(send, orders[step], odd)
            middle = summed.shape[0] // 2
            if step < 2:
                keep, send = summed[:middle], summed[middle:]
        done[odd].append(summed)
    halves = []
    for odd in range(2):
        current = jnp.stack(done[odd])
        for name in ("x1", "y1") if odd else ("x2", "y2"):
            middle = current.shape[1] // 2
            current = current[:, :middle] + swap(current[:, middle:], name, odd)
        halves.append(current)
    parts = jnp.concatenate(halves, axis=1)
    parts = jnp.concatenate([parts, parts[:1]], axis=0)
    slab = jnp.sum(lax.all_to_all(parts, "z_hi", 0, 0, tiled=True), axis=0)
    slabs = lax.all_to_all(
        jnp.broadcast_to(slab[None], (SLABS, UNIT, 128)), ("y", "z_lo"), 0, 0, tiled=True
    )
    pieces = inverse_root(where, slabs, factor)
    arrived = lax.all_to_all(pieces, ("core", "z_hi", "x"), 0, 0, tiled=True)
    return arrived.reshape(2, 16, 8, 128)[:, :12]


def solution(mesh):
    axes = ("z_lo", "core", "z_hi", "x", "y")
    fine = Mesh(mesh.devices.reshape(2, 2, 4, 4, 4), axes)
    return jax.shard_map(
        body,
        mesh=fine,
        in_specs=(P(axes, None, None, None),),
        out_specs=P(None, None, ("z_hi", "x", "y"), ("z_lo", "core")),
        check_vma=False,
    )
```

```python
import functools

import jax
import jax.numpy as jnp
from jax import lax
from jax.experimental import pallas as pl
from jax.experimental.pallas import tpu as pltpu
from jax.sharding import Mesh
from jax.sharding import PartitionSpec as P

ITERS = 4
SLABS = 8
UNIT = 136
LANES = (
    (("x1", "y1", "z", "x2", "y2"), False, ((0, 0, 88),)),
    (("x2", "y2", "z", "x1", "y1"), True, ((0, 88, 48), (1, 0, 40))),
    (("y1", "z", "x1", "x2", "y2"), False, ((1, 40, 80),)),
    (("y2", "z", "x2", "x1", "y1"), True, ((1, 120, 16), (2, 0, 64))),
    (("z", "x1", "y1", "x2", "y2"), False, ((2, 64, 72),)),
)
MIB = 1024 * 1024


def pieces_of(part):
    found, base = [], 0
    for lane, (_, _, pieces) in enumerate(LANES):
        for piece in pieces:
            if piece[0] == part:
                found.append((lane, base, piece[1], piece[2]))
                base += 32 * piece[2]
    return found


def place(order, flags):
    at = 0
    for name in order:
        at = at * 2 + flags[name]
    return at


def gram_kernel(part, where_ref, grads_ref, own_ref, away_ref):
    pieces = pieces_of(part)
    col_x, row_y, low_z, core = where_ref[0], where_ref[1], where_ref[2], where_ref[3]
    half = grads_ref.shape[-1] // 2
    slab_rows = half // SLABS
    rows = lax.broadcasted_iota(jnp.int32, (half, half), 0)
    cols = lax.broadcasted_iota(jnp.int32, (half, half), 1)
    upper = rows <= cols
    line_rows = lax.broadcasted_iota(jnp.int32, (slab_rows, 128), 0)
    line_cols = lax.broadcasted_iota(jnp.int32, (slab_rows, 128), 1)
    mult = functools.partial(jnp.dot, preferred_element_type=jnp.float32)
    spots = []
    for slab in range(SLABS):
        from_y = lax.bitwise_xor(row_y, slab // 2)
        high = lax.shift_right_logical(from_y, 1)
        flags = {
            "x1": 0,
            "x2": 0,
            "y1": lax.bitwise_xor(lax.bitwise_and(from_y, 1), high),
            "y2": high,
            "z": lax.bitwise_xor(low_z, slab % 2),
        }
        spots.append([place(LANES[lane][0], flags) for lane, _, _, _ in pieces])

    for step in range(4):
        relative = (step & 1) ^ (3 * (step >> 1))
        block = grads_ref[lax.bitwise_xor(col_x, relative)]
        flipped = block.T
        first = jnp.where(core == 0, block, flipped)
        second = jnp.where(core == 0, flipped, block)
        flags = {"x1": step & 1, "x2": step >> 1, "y1": 0, "y2": 0, "z": 0}
        bases = [base + place(LANES[lane][0], flags) * size for lane, base, _, size in pieces]
        for lhs, rhs, out_ref in ((second, first, away_ref), (first, second, own_ref)):
            corner = mult(lhs[:half], rhs[:, :half])
            right = mult(lhs, rhs[:, half:])
            cross, last = right[:half], right[half:]
            fold = jnp.where(upper, corner, last)
            for slab in range(SLABS):
                mine = slice(slab * slab_rows, (slab + 1) * slab_rows)
                near = slab * slab_rows // 128 * 128
                square = last[mine, near : near + 128]
                line = jnp.sum(
                    jnp.where(line_cols - line_rows == slab * slab_rows - near, square, 0.0), axis=0, keepdims=True
                )
                content = (
                    cross[mine, :128],
                    cross[mine, 128:],
                    fold[mine, :128],
                    fold[mine, 128:],
                    jnp.broadcast_to(line, (8, 128)),
                )
                for spot, base, (_, _, first_row, size) in zip(spots[slab], bases, pieces):
                    start = pl.multiple_of(spot * size + base, 8)
                    for band, value in enumerate(content):
                        low = max(band * slab_rows, first_row)
                        top = min(band * slab_rows + value.shape[0], first_row + size)
                        if low < top:
                            cut = value[low - band * slab_rows : top - band * slab_rows]
                            out_ref[pl.ds(start + low - first_row, top - low), :] = cut


def gram(part, where, grads):
    shape = jax.ShapeDtypeStruct((32 * UNIT, 128), jnp.float32)
    whole = pl.BlockSpec(memory_space=pltpu.VMEM)
    return pl.pallas_call(
        functools.partial(gram_kernel, part),
        out_shape=(shape, shape),
        in_specs=[pl.BlockSpec(memory_space=pltpu.SMEM), whole],
        out_specs=(whole, whole),
        compiler_params=pltpu.CompilerParams(vmem_limit_bytes=16 * MIB),
        name=f"gram_{part}",
    )(where, grads)


def split(value):
    high = value.astype(jnp.bfloat16)
    return high, (value - high.astype(jnp.float32)).astype(jnp.bfloat16)


def product(left, right):
    mult = functools.partial(jnp.dot, preferred_element_type=jnp.float32)
    return mult(left[0], right[0]) + (mult(left[0], right[1]) + mult(left[1], right[0]))


def root_kernel(factor, where_ref, slabs_ref, out_ref, full, picked):
    half = 256
    order = 2 * half
    slab_rows = half // SLABS
    rows = lax.broadcasted_iota(jnp.int32, (half, half), 0)
    cols = lax.broadcasted_iota(jnp.int32, (half, half), 1)

    def gathered(first):
        left = jnp.concatenate([slabs_ref[s, first : first + slab_rows] for s in range(SLABS)], axis=0)
        right = jnp.concatenate(
            [slabs_ref[s, first + slab_rows : first + 2 * slab_rows] for s in range(SLABS)], axis=0
        )
        return jnp.concatenate([left, right], axis=1) * factor

    cross = gathered(0)
    fold = gathered(64)
    line = jnp.concatenate(
        [sum(slabs_ref[s, 128:129] for s in group) for group in (range(4), range(4, 8))], axis=1
    )
    turned = fold.T
    corner = jnp.where(rows <= cols, fold, turned)
    last = jnp.where(rows > cols, fold, jnp.where(rows == cols, line * factor, turned))
    matrix = jnp.concatenate(
        [jnp.concatenate([corner, cross], axis=1), jnp.concatenate([cross.T, last], axis=1)], axis=0
    )
    total = jnp.sum(jnp.sum(matrix * matrix, axis=0, keepdims=True), axis=1, keepdims=True)
    scaling = 2.5 / jnp.sqrt(total)
    coupled = scaling * matrix
    identity = (
        lax.broadcasted_iota(jnp.int32, (order, order), 0) == lax.broadcasted_iota(jnp.int32, (order, order), 1)
    ).astype(jnp.float32)
    row_y, low_z = where_ref[1], where_ref[2]

    def mine(value):
        return jnp.where(low_z == 0, value[:, :half], value[:, half:])

    iterate = None
    for sweep in range(ITERS):
        step_matrix = (5.0 * identity - coupled) * 0.25
        if sweep == 0:
            full[...] = jnp.sqrt(jnp.sqrt(scaling)) * step_matrix
            for chunk in range(16):
                start = pl.multiple_of(32 * chunk + 8 * row_y, 8)
                picked[8 * chunk : 8 * chunk + 8, :] = full[pl.ds(start, 8), :]
            iterate = picked[...]
        else:
            iterate = product(split(iterate), split(step_matrix))
        if sweep < ITERS - 1:
            parts = split(step_matrix)
            squared = split(product(parts, parts))
            fourth = split(product(squared, squared))
            if sweep == ITERS - 2:
                coupled, identity = mine(coupled), mine(identity)
            coupled = product(fourth, split(coupled))
    for core in range(2):
        out_ref[16 * core : 16 * core + 16] = iterate[:, 128 * core : 128 * core + 128].reshape(16, 8, 128)


def inverse_root(where, slabs, factor):
    return pl.pallas_call(
        functools.partial(root_kernel, factor),
        out_shape=jax.ShapeDtypeStruct((32, 8, 128), jnp.float32),
        in_specs=[pl.BlockSpec(memory_space=pltpu.SMEM), pl.BlockSpec(memory_space=pltpu.VMEM)],
        out_specs=pl.BlockSpec(memory_space=pltpu.VMEM),
        scratch_shapes=[pltpu.VMEM((512, 512), jnp.float32), pltpu.VMEM((128, 512), jnp.float32)],
        compiler_params=pltpu.CompilerParams(vmem_limit_bytes=24 * MIB),
        name="inverse_root",
    )(where, slabs)


def swap(value, name, odd):
    if name in ("x1", "x2", "y1", "y2"):
        flip = 1 if name[1] == "1" else 3
        return lax.ppermute(value, name[0], [(i, i ^ flip) for i in range(4)])
    if not odd:
        return lax.ppermute(value, "z_lo", [(0, 1), (1, 0)])
    pairs = []
    for high in range(4):
        pairs += [(4 + high, (high + 1) % 4), ((high + 1) % 4, 4 + high)]
    return lax.ppermute(value, ("z_lo", "z_hi"), pairs)


def body(grads):
    local_grads = grads[0]
    order = local_grads.shape[1]
    where = jnp.stack([lax.axis_index(name).astype(jnp.int32) for name in ("x", "y", "z_lo", "core")])
    factor = 1.0 / (256 * order)
    waiting = local_grads
    kept, sent = [[] for _ in LANES], [[] for _ in LANES]
    for part in range(3):
        own, away = gram(part, where, waiting[4 * part : 4 * part + 4])
        waiting, away = lax.optimization_barrier((waiting, away))
        came = lax.ppermute(away, "core", [(0, 1), (1, 0)])
        for lane, base, _, size in pieces_of(part):
            for halves, first in ((kept, base), (sent, base + 16 * size)):
                rows = slice(first, first + 16 * size)
                halves[lane].append((own[rows] + came[rows]).reshape(16, size, 128))
    done = [[], []]
    for (order, odd, _), keep, send in zip(LANES, kept, sent):
        keep, send = (half[0] if len(half) == 1 else jnp.concatenate(half, axis=1) for half in (keep, send))
        for step in range(3):
            summed = keep + swap(send, order[step], odd)
            middle = summed.shape[0] // 2
            keep, send = summed[:middle], summed[middle:]
        done[odd].append(summed)
    even, odd = (jnp.concatenate(lanes, axis=1) for lanes in done)
    for along in ("x", "y"):
        middle = even.shape[0] // 2
        even_keep, odd_keep, even_send, odd_send = lax.optimization_barrier(
            (even[:middle], odd[:middle], even[middle:], odd[middle:])
        )
        even_came, odd_came = lax.optimization_barrier(
            (swap(even_send, along + "2", False), swap(odd_send, along + "1", True))
        )
        even, odd = even_keep + even_came, odd_keep + odd_came
    even, odd = even[0], odd[0]
    held = {}
    for lanes, total in ((LANES[0::2], even), (LANES[1::2], odd)):
        first = 0
        for _, _, pieces in lanes:
            for piece in pieces:
                held[piece[:2]] = total[first : first + piece[2]]
                first += piece[2]
    parts = [jnp.concatenate([held[key] for key in sorted(held) if key[0] == part]) for part in range(3)]
    parts = jnp.stack(parts + parts[:1])
    high_z = lax.axis_index("z_hi")
    pick = [lax.dynamic_index_in_dim(parts, lax.bitwise_xor(high_z, k), 0, False) for k in range(4)]
    slab = pick[0] + sum(lax.ppermute(pick[k], "z_hi", [(i, i ^ k) for i in range(4)]) for k in (2, 1, 3))
    slabs = lax.all_to_all(
        jnp.broadcast_to(slab[None], (SLABS, UNIT, 128)), ("y", "z_lo"), 0, 0, tiled=True
    )
    pieces = inverse_root(where, slabs, factor)
    arrived = lax.all_to_all(pieces, ("core", "z_hi", "x"), 0, 0, tiled=True)
    return arrived.reshape(2, 16, 8, 128)[:, :12]


def solution(mesh):
    axes = ("z_lo", "core", "z_hi", "x", "y")
    fine = Mesh(mesh.devices.reshape(2, 2, 4, 4, 4), axes)
    return jax.shard_map(
        body,
        mesh=fine,
        in_specs=(P(axes, None, None, None),),
        out_specs=P(None, None, ("z_hi", "x", "y"), ("z_lo", "core")),
        check_vma=False,
    )
```

```python
import functools

import jax
import jax.numpy as jnp
from jax import lax
from jax.experimental import pallas as pl
from jax.experimental.pallas import tpu as pltpu
from jax.sharding import Mesh
from jax.sharding import PartitionSpec as P

ITERS = 4
SLABS = 8
UNIT = 136
LANES = (
    (("x1", "y1", "z", "x2", "y2"), False, ((0, 0, 80),)),
    (("x2", "y2", "z", "x1", "y1"), True, ((0, 80, 56), (1, 0, 24),)),
    (("y1", "z", "x1", "x2", "y2"), False, ((1, 24, 88),)),
    (("y2", "z", "x2", "x1", "y1"), True, ((1, 112, 24), (2, 0, 56),)),
    (("z", "x2", "y2", "x1", "y1"), False, ((2, 56, 80),)),
)
MIB = 1024 * 1024


def pieces_of(part):
    found, base = [], 0
    for lane, (_, _, pieces) in enumerate(LANES):
        for piece in pieces:
            if piece[0] == part:
                found.append((lane, base, piece[1], piece[2]))
                base += 32 * piece[2]
    return found


def place(order, flags):
    at = 0
    for name in order:
        at = at * 2 + flags[name]
    return at


def gram_kernel(part, where_ref, grads_ref, own_ref, away_ref):
    pieces = pieces_of(part)
    col_x, row_y, low_z, core = where_ref[0], where_ref[1], where_ref[2], where_ref[3]
    half = grads_ref.shape[-1] // 2
    slab_rows = half // SLABS
    rows = lax.broadcasted_iota(jnp.int32, (half, half), 0)
    cols = lax.broadcasted_iota(jnp.int32, (half, half), 1)
    upper = rows <= cols
    line_rows = lax.broadcasted_iota(jnp.int32, (slab_rows, 128), 0)
    line_cols = lax.broadcasted_iota(jnp.int32, (slab_rows, 128), 1)
    mult = functools.partial(jnp.dot, preferred_element_type=jnp.float32)
    spots = []
    for slab in range(SLABS):
        from_y = lax.bitwise_xor(row_y, slab // 2)
        high = lax.shift_right_logical(from_y, 1)
        flags = {
            "x1": 0,
            "x2": 0,
            "y1": lax.bitwise_xor(lax.bitwise_and(from_y, 1), high),
            "y2": high,
            "z": lax.bitwise_xor(low_z, slab % 2),
        }
        spots.append([place(LANES[lane][0], flags) for lane, _, _, _ in pieces])

    for step in range(4):
        relative = (step & 1) ^ (3 * (step >> 1))
        block = grads_ref[lax.bitwise_xor(col_x, relative)]
        flipped = block.T
        first = jnp.where(core == 0, block, flipped)
        second = jnp.where(core == 0, flipped, block)
        flags = {"x1": step & 1, "x2": step >> 1, "y1": 0, "y2": 0, "z": 0}
        bases = [base + place(LANES[lane][0], flags) * size for lane, base, _, size in pieces]
        for lhs, rhs, out_ref in ((second, first, away_ref), (first, second, own_ref)):
            corner = mult(lhs[:half], rhs[:, :half])
            right = mult(lhs, rhs[:, half:])
            cross, last = right[:half], right[half:]
            fold = jnp.where(upper, corner, last)
            for slab in range(SLABS):
                mine = slice(slab * slab_rows, (slab + 1) * slab_rows)
                near = slab * slab_rows // 128 * 128
                square = last[mine, near : near + 128]
                line = jnp.sum(
                    jnp.where(line_cols - line_rows == slab * slab_rows - near, square, 0.0), axis=0, keepdims=True
                )
                content = (
                    cross[mine, :128],
                    cross[mine, 128:],
                    fold[mine, :128],
                    fold[mine, 128:],
                    jnp.broadcast_to(line, (8, 128)),
                )
                for spot, base, (_, _, first_row, size) in zip(spots[slab], bases, pieces):
                    start = pl.multiple_of(spot * size + base, 8)
                    for band, value in enumerate(content):
                        low = max(band * slab_rows, first_row)
                        top = min(band * slab_rows + value.shape[0], first_row + size)
                        if low < top:
                            cut = value[low - band * slab_rows : top - band * slab_rows]
                            out_ref[pl.ds(start + low - first_row, top - low), :] = cut


def gram(part, where, grads):
    shape = jax.ShapeDtypeStruct((32 * UNIT, 128), jnp.float32)
    whole = pl.BlockSpec(memory_space=pltpu.VMEM)
    return pl.pallas_call(
        functools.partial(gram_kernel, part),
        out_shape=(shape, shape),
        in_specs=[pl.BlockSpec(memory_space=pltpu.SMEM), whole],
        out_specs=(whole, whole),
        compiler_params=pltpu.CompilerParams(vmem_limit_bytes=16 * MIB),
        name=f"gram_{part}",
    )(where, grads)


def split(value):
    high = value.astype(jnp.bfloat16)
    return high, (value - high.astype(jnp.float32)).astype(jnp.bfloat16)


def product(left, right):
    mult = functools.partial(jnp.dot, preferred_element_type=jnp.float32)
    return mult(left[0], right[0]) + (mult(left[0], right[1]) + mult(left[1], right[0]))


def symmetric(left, right):
    top = product([half[:256] for half in left], right)
    last = product([half[256:] for half in left], [half[:, 256:] for half in right])
    return jnp.concatenate([top, jnp.concatenate([top[:, 256:].T, last], axis=1)], axis=0)


def square(parts):
    mult = functools.partial(jnp.dot, preferred_element_type=jnp.float32)
    high, low = parts
    mixed = mult(high, low)
    top = mult(high[:256], high)
    last = mult(high[256:], high[:, 256:])
    first = top[:, :256] + (mixed[:256, :256] + mixed[:256, :256].T)
    cross = top[:, 256:] + (mixed[:256, 256:] + mixed[256:, :256].T)
    last = last + (mixed[256:, 256:] + mixed[256:, 256:].T)
    return jnp.concatenate(
        [jnp.concatenate([first, cross], axis=1), jnp.concatenate([cross.T, last], axis=1)], axis=0
    )


def root_kernel(factor, where_ref, slabs_ref, out_ref, full, picked):
    half = 256
    order = 2 * half
    slab_rows = half // SLABS
    rows = lax.broadcasted_iota(jnp.int32, (half, half), 0)
    cols = lax.broadcasted_iota(jnp.int32, (half, half), 1)

    def gathered(first):
        left = jnp.concatenate([slabs_ref[s, first : first + slab_rows] for s in range(SLABS)], axis=0)
        right = jnp.concatenate(
            [slabs_ref[s, first + slab_rows : first + 2 * slab_rows] for s in range(SLABS)], axis=0
        )
        return jnp.concatenate([left, right], axis=1) * factor

    cross = gathered(0)
    fold = gathered(64)
    line = jnp.concatenate(
        [sum(slabs_ref[s, 128:129] for s in group) for group in (range(4), range(4, 8))], axis=1
    )
    turned = fold.T
    corner = jnp.where(rows <= cols, fold, turned)
    last = jnp.where(rows > cols, fold, jnp.where(rows == cols, line * factor, turned))
    matrix = jnp.concatenate(
        [jnp.concatenate([corner, cross], axis=1), jnp.concatenate([cross.T, last], axis=1)], axis=0
    )
    total = jnp.sum(jnp.sum(matrix * matrix, axis=0, keepdims=True), axis=1, keepdims=True)
    scaling = 2.5 / jnp.sqrt(total)
    coupled = scaling * matrix
    identity = (
        lax.broadcasted_iota(jnp.int32, (order, order), 0) == lax.broadcasted_iota(jnp.int32, (order, order), 1)
    ).astype(jnp.float32)
    row_y, low_z = where_ref[1], where_ref[2]

    def mine(value):
        return jnp.where(low_z == 0, value[:, :half], value[:, half:])

    iterate = None
    for sweep in range(ITERS):
        step_matrix = (5.0 * identity - coupled) * 0.25
        if sweep == 0:
            full[...] = jnp.sqrt(jnp.sqrt(scaling)) * step_matrix
            for chunk in range(16):
                start = pl.multiple_of(32 * chunk + 8 * row_y, 8)
                picked[8 * chunk : 8 * chunk + 8, :] = full[pl.ds(start, 8), :]
            iterate = picked[...]
        else:
            iterate = product(split(iterate), split(step_matrix))
        if sweep < ITERS - 1:
            parts = split(step_matrix)
            squared = split(square(parts))
            fourth = split(square(squared))
            if sweep == ITERS - 2:
                coupled, identity = mine(coupled), mine(identity)
                coupled = product(fourth, split(coupled))
            else:
                coupled = symmetric(fourth, split(coupled))
    for core in range(2):
        out_ref[16 * core : 16 * core + 16] = iterate[:, 128 * core : 128 * core + 128].reshape(16, 8, 128)


def inverse_root(where, slabs, factor):
    return pl.pallas_call(
        functools.partial(root_kernel, factor),
        out_shape=jax.ShapeDtypeStruct((32, 8, 128), jnp.float32),
        in_specs=[pl.BlockSpec(memory_space=pltpu.SMEM), pl.BlockSpec(memory_space=pltpu.VMEM)],
        out_specs=pl.BlockSpec(memory_space=pltpu.VMEM),
        scratch_shapes=[pltpu.VMEM((512, 512), jnp.float32), pltpu.VMEM((128, 512), jnp.float32)],
        compiler_params=pltpu.CompilerParams(vmem_limit_bytes=24 * MIB),
        name="inverse_root",
    )(where, slabs)


def swap(value, name, odd):
    if name in ("x1", "x2", "y1", "y2"):
        flip = 1 if name[1] == "1" else 3
        return lax.ppermute(value, name[0], [(i, i ^ flip) for i in range(4)])
    if not odd:
        return lax.ppermute(value, "z_lo", [(0, 1), (1, 0)])
    pairs = []
    for high in range(4):
        pairs += [(4 + high, (high + 1) % 4), ((high + 1) % 4, 4 + high)]
    return lax.ppermute(value, ("z_lo", "z_hi"), pairs)


def after(value, before):
    return lax.optimization_barrier((value, before))[0]


def body(grads):
    local_grads = grads[0]
    order = local_grads.shape[1]
    where = jnp.stack([lax.axis_index(name).astype(jnp.int32) for name in ("x", "y", "z_lo", "core")])
    factor = 1.0 / (256 * order)
    own, came, keeps, sends = [], [], [], []

    def enter(part):
        blocks = local_grads[4 * part : 4 * part + 4]
        if part:
            blocks = after(local_grads, away_of[-1])[4 * part : 4 * part + 4]
        stays, away = gram(part, where, blocks)
        away_of.append(away)
        own.append(stays)
        came.append(lax.ppermute(away, "core", [(0, 1), (1, 0)]))

    def depart(lane):
        halves = [[], []]
        for part in range(3):
            for which, base, _, size in pieces_of(part):
                if which == lane:
                    other = came[part]
                    for half, first in zip(halves, (base, base + 16 * size)):
                        rows = slice(first, first + 16 * size)
                        half.append((own[part][rows] + other[rows]).reshape(16, size, 128))
        keep, send = (half[0] if len(half) == 1 else jnp.concatenate(half, axis=1) for half in halves)
        keeps.append(keep)
        sends.append(send)

    away_of = []
    enter(0)
    enter(1)
    depart(0)
    enter(2)
    for lane in range(1, len(LANES)):
        depart(lane)
    for step in range(3):
        for lane, (order, odd, _) in enumerate(LANES):
            summed = keeps[lane] + swap(sends[lane], order[step], odd)
            middle = summed.shape[0] // 2
            keeps[lane], sends[lane] = summed[:middle], summed[middle:]
    done = [[], []]
    for (order, _, _), keep, send in zip(LANES, keeps, sends):
        done[order[3] == "x1"].append(jnp.concatenate([keep, send]))
    even, odd = (jnp.concatenate(lanes, axis=1) for lanes in done)
    for along in ("x", "y"):
        middle = even.shape[0] // 2
        even_keep, odd_keep, even_send, odd_send = lax.optimization_barrier(
            (even[:middle], odd[:middle], even[middle:], odd[middle:])
        )
        even_came, odd_came = lax.optimization_barrier(
            (swap(even_send, along + "2", False), swap(odd_send, along + "1", True))
        )
        even, odd = even_keep + even_came, odd_keep + odd_came
    even, odd = even[0], odd[0]
    held = {}
    for total, last in ((even, "x2"), (odd, "x1")):
        first = 0
        for order, _, pieces in LANES:
            if order[3] != last:
                continue
            for piece in pieces:
                held[piece[:2]] = total[first : first + piece[2]]
                first += piece[2]
    parts = [jnp.concatenate([held[key] for key in sorted(held) if key[0] == part]) for part in range(3)]
    parts = jnp.stack(parts + parts[:1])
    high_z = lax.axis_index("z_hi")
    pick = [lax.dynamic_index_in_dim(parts, lax.bitwise_xor(high_z, k), 0, False) for k in range(4)]
    slab = pick[0] + sum(lax.ppermute(pick[k], "z_hi", [(i, i ^ k) for i in range(4)]) for k in (2, 1, 3))
    slabs = lax.all_to_all(
        jnp.broadcast_to(slab[None], (SLABS, UNIT, 128)), ("y", "z_lo"), 0, 0, tiled=True
    )
    pieces = inverse_root(where, slabs, factor)
    arrived = lax.all_to_all(pieces, ("core", "z_hi", "x"), 0, 0, tiled=True)
    return arrived.reshape(2, 16, 8, 128)[:, :12]


def solution(mesh):
    axes = ("z_lo", "core", "z_hi", "x", "y")
    fine = Mesh(mesh.devices.reshape(2, 2, 4, 4, 4), axes)
    return jax.shard_map(
        body,
        mesh=fine,
        in_specs=(P(axes, None, None, None),),
        out_specs=P(None, None, ("z_hi", "x", "y"), ("z_lo", "core")),
        check_vma=False,
    )
```

```python
import functools

import jax
import jax.numpy as jnp
from jax import lax
from jax.experimental import pallas as pl
from jax.experimental.pallas import tpu as pltpu
from jax.sharding import Mesh
from jax.sharding import PartitionSpec as P

ITERS = 4
SLABS = 8
UNIT = 136
LANES = (
    (("x1", "y1", "z", "x2", "y2"), False, ((0, 0, 88),)),
    (("x2", "y2", "z", "x1", "y1"), True, ((0, 88, 48), (1, 0, 32),)),
    (("y1", "z", "x1", "x2", "y2"), False, ((1, 32, 80),)),
    (("y2", "z", "x2", "x1", "y1"), True, ((1, 112, 24), (2, 0, 56),)),
    (("z", "x2", "y2", "x1", "y1"), False, ((2, 56, 80),)),
)
MIB = 1024 * 1024


def pieces_of(part):
    found, base = [], 0
    for lane, (_, _, pieces) in enumerate(LANES):
        for piece in pieces:
            if piece[0] == part:
                found.append((lane, base, piece[1], piece[2]))
                base += 32 * piece[2]
    return found


def place(order, flags):
    at = 0
    for name in order:
        at = at * 2 + flags[name]
    return at


def gram_kernel(part, where_ref, grads_ref, own_ref, away_ref):
    pieces = pieces_of(part)
    col_x, row_y, low_z, core = where_ref[0], where_ref[1], where_ref[2], where_ref[3]
    half = grads_ref.shape[-1] // 2
    slab_rows = half // SLABS
    rows = lax.broadcasted_iota(jnp.int32, (half, half), 0)
    cols = lax.broadcasted_iota(jnp.int32, (half, half), 1)
    upper = rows <= cols
    line_rows = lax.broadcasted_iota(jnp.int32, (slab_rows, 128), 0)
    line_cols = lax.broadcasted_iota(jnp.int32, (slab_rows, 128), 1)
    mult = functools.partial(jnp.dot, preferred_element_type=jnp.float32)
    spots = []
    for slab in range(SLABS):
        from_y = lax.bitwise_xor(row_y, slab // 2)
        high = lax.shift_right_logical(from_y, 1)
        flags = {
            "x1": 0,
            "x2": 0,
            "y1": lax.bitwise_xor(lax.bitwise_and(from_y, 1), high),
            "y2": high,
            "z": lax.bitwise_xor(low_z, slab % 2),
        }
        spots.append([place(LANES[lane][0], flags) for lane, _, _, _ in pieces])

    for step in range(4):
        relative = (step & 1) ^ (3 * (step >> 1))
        block = grads_ref[lax.bitwise_xor(col_x, relative)]
        flipped = block.T
        first = jnp.where(core == 0, block, flipped)
        second = jnp.where(core == 0, flipped, block)
        flags = {"x1": step & 1, "x2": step >> 1, "y1": 0, "y2": 0, "z": 0}
        bases = [base + place(LANES[lane][0], flags) * size for lane, base, _, size in pieces]
        for lhs, rhs, out_ref in ((second, first, away_ref), (first, second, own_ref)):
            corner = mult(lhs[:half], rhs[:, :half])
            right = mult(lhs, rhs[:, half:])
            cross, last = right[:half], right[half:]
            fold = jnp.where(upper, corner, last)
            for slab in range(SLABS):
                mine = slice(slab * slab_rows, (slab + 1) * slab_rows)
                near = slab * slab_rows // 128 * 128
                square = last[mine, near : near + 128]
                line = jnp.sum(
                    jnp.where(line_cols - line_rows == slab * slab_rows - near, square, 0.0), axis=0, keepdims=True
                )
                content = (
                    cross[mine, :128],
                    cross[mine, 128:],
                    fold[mine, :128],
                    fold[mine, 128:],
                    jnp.broadcast_to(line, (8, 128)),
                )
                for spot, base, (_, _, first_row, size) in zip(spots[slab], bases, pieces):
                    start = pl.multiple_of(spot * size + base, 8)
                    for band, value in enumerate(content):
                        low = max(band * slab_rows, first_row)
                        top = min(band * slab_rows + value.shape[0], first_row + size)
                        if low < top:
                            cut = value[low - band * slab_rows : top - band * slab_rows]
                            out_ref[pl.ds(start + low - first_row, top - low), :] = cut


def gram(part, where, grads):
    shape = jax.ShapeDtypeStruct((32 * UNIT, 128), jnp.float32)
    whole = pl.BlockSpec(memory_space=pltpu.VMEM)
    return pl.pallas_call(
        functools.partial(gram_kernel, part),
        out_shape=(shape, shape),
        in_specs=[pl.BlockSpec(memory_space=pltpu.SMEM), whole],
        out_specs=(whole, whole),
        compiler_params=pltpu.CompilerParams(vmem_limit_bytes=16 * MIB),
        name=f"gram_{part}",
    )(where, grads)


def split(value):
    high = value.astype(jnp.bfloat16)
    return high, (value - high.astype(jnp.float32)).astype(jnp.bfloat16)


def product(left, right):
    mult = functools.partial(jnp.dot, preferred_element_type=jnp.float32)
    return mult(left[0], right[0]) + (mult(left[0], right[1]) + mult(left[1], right[0]))


def symmetric(left, right):
    top = product([half[:256] for half in left], right)
    last = product([half[256:] for half in left], [half[:, 256:] for half in right])
    return jnp.concatenate([top, jnp.concatenate([top[:, 256:].T, last], axis=1)], axis=0)


def square(parts):
    mult = functools.partial(jnp.dot, preferred_element_type=jnp.float32)
    high, low = parts
    mixed = mult(high, low)
    top = mult(high[:256], high)
    last = mult(high[256:], high[:, 256:])
    first = top[:, :256] + (mixed[:256, :256] + mixed[:256, :256].T)
    cross = top[:, 256:] + (mixed[:256, 256:] + mixed[256:, :256].T)
    last = last + (mixed[256:, 256:] + mixed[256:, 256:].T)
    return jnp.concatenate(
        [jnp.concatenate([first, cross], axis=1), jnp.concatenate([cross.T, last], axis=1)], axis=0
    )


def root_kernel(factor, where_ref, slabs_ref, out_ref, full, picked):
    half = 256
    order = 2 * half
    slab_rows = half // SLABS
    rows = lax.broadcasted_iota(jnp.int32, (half, half), 0)
    cols = lax.broadcasted_iota(jnp.int32, (half, half), 1)

    def gathered(first):
        left = jnp.concatenate([slabs_ref[s, first : first + slab_rows] for s in range(SLABS)], axis=0)
        right = jnp.concatenate(
            [slabs_ref[s, first + slab_rows : first + 2 * slab_rows] for s in range(SLABS)], axis=0
        )
        return jnp.concatenate([left, right], axis=1) * factor

    cross = gathered(0)
    fold = gathered(64)
    line = jnp.concatenate(
        [sum(slabs_ref[s, 128:129] for s in group) for group in (range(4), range(4, 8))], axis=1
    )
    turned = fold.T
    corner = jnp.where(rows <= cols, fold, turned)
    last = jnp.where(rows > cols, fold, jnp.where(rows == cols, line * factor, turned))
    matrix = jnp.concatenate(
        [jnp.concatenate([corner, cross], axis=1), jnp.concatenate([cross.T, last], axis=1)], axis=0
    )
    total = jnp.sum(jnp.sum(matrix * matrix, axis=0, keepdims=True), axis=1, keepdims=True)
    scaling = 2.5 / jnp.sqrt(total)
    coupled = scaling * matrix
    identity = (
        lax.broadcasted_iota(jnp.int32, (order, order), 0) == lax.broadcasted_iota(jnp.int32, (order, order), 1)
    ).astype(jnp.float32)
    row_y, low_z = where_ref[1], where_ref[2]

    def mine(value):
        return jnp.where(low_z == 0, value[:, :half], value[:, half:])

    iterate = None
    for sweep in range(ITERS):
        step_matrix = (5.0 * identity - coupled) * 0.25
        if sweep == 0:
            full[...] = jnp.sqrt(jnp.sqrt(scaling)) * step_matrix
            for chunk in range(16):
                start = pl.multiple_of(32 * chunk + 8 * row_y, 8)
                picked[8 * chunk : 8 * chunk + 8, :] = full[pl.ds(start, 8), :]
            iterate = picked[...]
        else:
            iterate = product(split(iterate), split(step_matrix))
        if sweep < ITERS - 1:
            parts = split(step_matrix)
            squared = split(square(parts))
            fourth = split(square(squared))
            if sweep == ITERS - 2:
                coupled, identity = mine(coupled), mine(identity)
                coupled = product(fourth, split(coupled))
            else:
                coupled = symmetric(fourth, split(coupled))
    for core in range(2):
        out_ref[16 * core : 16 * core + 16] = iterate[:, 128 * core : 128 * core + 128].reshape(16, 8, 128)


def inverse_root(where, slabs, factor):
    return pl.pallas_call(
        functools.partial(root_kernel, factor),
        out_shape=jax.ShapeDtypeStruct((32, 8, 128), jnp.float32),
        in_specs=[pl.BlockSpec(memory_space=pltpu.SMEM), pl.BlockSpec(memory_space=pltpu.VMEM)],
        out_specs=pl.BlockSpec(memory_space=pltpu.VMEM),
        scratch_shapes=[pltpu.VMEM((512, 512), jnp.float32), pltpu.VMEM((128, 512), jnp.float32)],
        compiler_params=pltpu.CompilerParams(vmem_limit_bytes=24 * MIB),
        name="inverse_root",
    )(where, slabs)


def swap(value, name, odd):
    if name in ("x1", "x2", "y1", "y2"):
        flip = 1 if name[1] == "1" else 3
        return lax.ppermute(value, name[0], [(i, i ^ flip) for i in range(4)])
    if not odd:
        return lax.ppermute(value, "z_lo", [(0, 1), (1, 0)])
    pairs = []
    for high in range(4):
        pairs += [(4 + high, (high + 1) % 4), ((high + 1) % 4, 4 + high)]
    return lax.ppermute(value, ("z_lo", "z_hi"), pairs)


def after(value, before):
    return lax.optimization_barrier((value, before))[0]


def body(grads):
    local_grads = grads[0]
    order = local_grads.shape[1]
    where = jnp.stack([lax.axis_index(name).astype(jnp.int32) for name in ("x", "y", "z_lo", "core")])
    factor = 1.0 / (256 * order)
    own, came, keeps, sends = [], [], [], []

    def enter(part):
        blocks = local_grads[4 * part : 4 * part + 4]
        if part:
            blocks = after(local_grads, away_of[-1])[4 * part : 4 * part + 4]
        stays, away = gram(part, where, blocks)
        away_of.append(away)
        own.append(stays)
        came.append(lax.ppermute(away, "core", [(0, 1), (1, 0)]))

    def depart(lane):
        halves = [[], []]
        for part in range(3):
            for which, base, _, size in pieces_of(part):
                if which == lane:
                    other = came[part]
                    for half, first in zip(halves, (base, base + 16 * size)):
                        rows = slice(first, first + 16 * size)
                        half.append((own[part][rows] + other[rows]).reshape(16, size, 128))
        keep, send = (half[0] if len(half) == 1 else jnp.concatenate(half, axis=1) for half in halves)
        keeps.append(keep)
        sends.append(send)

    away_of = []
    enter(0)
    enter(1)
    depart(0)
    enter(2)
    for lane in range(1, len(LANES)):
        depart(lane)
    for step in range(3):
        for lane, (order, odd, _) in enumerate(LANES):
            summed = keeps[lane] + swap(sends[lane], order[step], odd)
            middle = summed.shape[0] // 2
            keeps[lane], sends[lane] = summed[:middle], summed[middle:]
    done = [[], []]
    for (order, _, _), keep, send in zip(LANES, keeps, sends):
        done[order[3] == "x1"].append(jnp.concatenate([keep, send]))
    even, odd = (jnp.concatenate(lanes, axis=1) for lanes in done)
    for along in ("x", "y"):
        middle = even.shape[0] // 2
        even_keep, even_send = lax.optimization_barrier((even[:middle], even[middle:]))
        odd_keep, odd_send = lax.optimization_barrier((odd[:middle], odd[middle:]))
        even_came, odd_came = lax.optimization_barrier(
            (swap(even_send, along + "2", False), swap(odd_send, along + "1", True))
        )
        even, odd = even_keep + even_came, odd_keep + odd_came
    even, odd = even[0], odd[0]
    held = {}
    for total, last in ((even, "x2"), (odd, "x1")):
        first = 0
        for order, _, pieces in LANES:
            if order[3] != last:
                continue
            for piece in pieces:
                held[piece[:2]] = total[first : first + piece[2]]
                first += piece[2]
    parts = [jnp.concatenate([held[key] for key in sorted(held) if key[0] == part]) for part in range(3)]
    parts = jnp.stack(parts + parts[:1])
    high_z = lax.axis_index("z_hi")
    pick = [lax.dynamic_index_in_dim(parts, lax.bitwise_xor(high_z, k), 0, False) for k in range(4)]
    slab = pick[0] + sum(lax.ppermute(pick[k], "z_hi", [(i, i ^ k) for i in range(4)]) for k in (2, 1, 3))
    slabs = lax.all_to_all(
        jnp.broadcast_to(slab[None], (SLABS, UNIT, 128)), ("y", "z_lo"), 0, 0, tiled=True
    )
    pieces = inverse_root(where, slabs, factor)
    arrived = lax.all_to_all(pieces, ("core", "z_hi", "x"), 0, 0, tiled=True)
    return arrived.reshape(2, 16, 8, 128)[:, :12]


def solution(mesh):
    axes = ("z_lo", "core", "z_hi", "x", "y")
    fine = Mesh(mesh.devices.reshape(2, 2, 4, 4, 4), axes)
    return jax.shard_map(
        body,
        mesh=fine,
        in_specs=(P(axes, None, None, None),),
        out_specs=P(None, None, ("z_hi", "x", "y"), ("z_lo", "core")),
        check_vma=False,
    )
```

```python
import functools

import jax
import jax.numpy as jnp
from jax import lax
from jax.experimental import pallas as pl
from jax.experimental.pallas import tpu as pltpu
from jax.sharding import Mesh
from jax.sharding import PartitionSpec as P

ITERS = 4
SLABS = 8
UNIT = 136
LANES = (
    (("x1", "y1", "z", "x2", "y2"), False, ((0, 0, 88),)),
    (("x2", "y2", "z", "x1", "y1"), True, ((0, 88, 48), (1, 0, 32),)),
    (("y1", "z", "x1", "x2", "y2"), False, ((1, 32, 80),)),
    (("y2", "z", "x2", "x1", "y1"), True, ((1, 112, 24), (2, 0, 56),)),
    (("z", "x2", "y2", "x1", "y1"), False, ((2, 56, 80),)),
)
MIB = 1024 * 1024


def pieces_of(part):
    found, base = [], 0
    for lane, (_, _, pieces) in enumerate(LANES):
        for piece in pieces:
            if piece[0] == part:
                found.append((lane, base, piece[1], piece[2]))
                base += 32 * piece[2]
    return found


def place(order, flags):
    at = 0
    for name in order:
        at = at * 2 + flags[name]
    return at


def gram_kernel(part, where_ref, grads_ref, own_ref, away_ref):
    pieces = pieces_of(part)
    col_x, row_y, low_z, core = where_ref[0], where_ref[1], where_ref[2], where_ref[3]
    half = grads_ref.shape[-1] // 2
    slab_rows = half // SLABS
    rows = lax.broadcasted_iota(jnp.int32, (half, half), 0)
    cols = lax.broadcasted_iota(jnp.int32, (half, half), 1)
    upper = rows <= cols
    line_rows = lax.broadcasted_iota(jnp.int32, (slab_rows, 128), 0)
    line_cols = lax.broadcasted_iota(jnp.int32, (slab_rows, 128), 1)
    mult = functools.partial(jnp.dot, preferred_element_type=jnp.float32)
    spots = []
    for slab in range(SLABS):
        from_y = lax.bitwise_xor(row_y, slab // 2)
        high = lax.shift_right_logical(from_y, 1)
        flags = {
            "x1": 0,
            "x2": 0,
            "y1": lax.bitwise_xor(lax.bitwise_and(from_y, 1), high),
            "y2": high,
            "z": lax.bitwise_xor(low_z, slab % 2),
        }
        spots.append([place(LANES[lane][0], flags) for lane, _, _, _ in pieces])

    for step in range(4):
        relative = (step & 1) ^ (3 * (step >> 1))
        block = grads_ref[lax.bitwise_xor(col_x, relative)]
        flipped = block.T
        first = jnp.where(core == 0, block, flipped)
        second = jnp.where(core == 0, flipped, block)
        flags = {"x1": step & 1, "x2": step >> 1, "y1": 0, "y2": 0, "z": 0}
        bases = [base + place(LANES[lane][0], flags) * size for lane, base, _, size in pieces]
        for lhs, rhs, out_ref in ((second, first, away_ref), (first, second, own_ref)):
            corner = mult(lhs[:half], rhs[:, :half])
            right = mult(lhs, rhs[:, half:])
            cross, last = right[:half], right[half:]
            fold = jnp.where(upper, corner, last)
            for slab in range(SLABS):
                mine = slice(slab * slab_rows, (slab + 1) * slab_rows)
                near = slab * slab_rows // 128 * 128
                square = last[mine, near : near + 128]
                line = jnp.sum(
                    jnp.where(line_cols - line_rows == slab * slab_rows - near, square, 0.0), axis=0, keepdims=True
                )
                content = (
                    cross[mine, :128],
                    cross[mine, 128:],
                    fold[mine, :128],
                    fold[mine, 128:],
                    jnp.broadcast_to(line, (8, 128)),
                )
                for spot, base, (_, _, first_row, size) in zip(spots[slab], bases, pieces):
                    start = pl.multiple_of(spot * size + base, 8)
                    for band, value in enumerate(content):
                        low = max(band * slab_rows, first_row)
                        top = min(band * slab_rows + value.shape[0], first_row + size)
                        if low < top:
                            cut = value[low - band * slab_rows : top - band * slab_rows]
                            out_ref[pl.ds(start + low - first_row, top - low), :] = cut


def gram(part, where, grads):
    shape = jax.ShapeDtypeStruct((32 * UNIT, 128), jnp.float32)
    whole = pl.BlockSpec(memory_space=pltpu.VMEM)
    return pl.pallas_call(
        functools.partial(gram_kernel, part),
        out_shape=(shape, shape),
        in_specs=[pl.BlockSpec(memory_space=pltpu.SMEM), whole],
        out_specs=(whole, whole),
        compiler_params=pltpu.CompilerParams(vmem_limit_bytes=16 * MIB),
        name=f"gram_{part}",
    )(where, grads)


def split(value):
    high = value.astype(jnp.bfloat16)
    return high, (value - high.astype(jnp.float32)).astype(jnp.bfloat16)


def product(left, right):
    mult = functools.partial(jnp.dot, preferred_element_type=jnp.float32)
    return mult(left[0], right[0]) + (mult(left[0], right[1]) + mult(left[1], right[0]))


def symmetric(left, right):
    top = product([half[:256] for half in left], right)
    last = product([half[256:] for half in left], [half[:, 256:] for half in right])
    return jnp.concatenate([top, jnp.concatenate([top[:, 256:].T, last], axis=1)], axis=0)


def square(parts):
    mult = functools.partial(jnp.dot, preferred_element_type=jnp.float32)
    high, low = parts
    mixed = mult(high, low)
    top = mult(high[:256], high)
    last = mult(high[256:], high[:, 256:])
    first = top[:, :256] + (mixed[:256, :256] + mixed[:256, :256].T)
    cross = top[:, 256:] + (mixed[:256, 256:] + mixed[256:, :256].T)
    last = last + (mixed[256:, 256:] + mixed[256:, 256:].T)
    return jnp.concatenate(
        [jnp.concatenate([first, cross], axis=1), jnp.concatenate([cross.T, last], axis=1)], axis=0
    )


def root_kernel(factor, where_ref, slabs_ref, out_ref, full, picked):
    half = 256
    order = 2 * half
    slab_rows = half // SLABS
    rows = lax.broadcasted_iota(jnp.int32, (half, half), 0)
    cols = lax.broadcasted_iota(jnp.int32, (half, half), 1)

    def gathered(first):
        left = jnp.concatenate([slabs_ref[s, first : first + slab_rows] for s in range(SLABS)], axis=0)
        right = jnp.concatenate(
            [slabs_ref[s, first + slab_rows : first + 2 * slab_rows] for s in range(SLABS)], axis=0
        )
        return jnp.concatenate([left, right], axis=1) * factor

    cross = gathered(0)
    fold = gathered(64)
    line = jnp.concatenate(
        [sum(slabs_ref[s, 128:129] for s in group) for group in (range(4), range(4, 8))], axis=1
    )
    turned = fold.T
    corner = jnp.where(rows <= cols, fold, turned)
    last = jnp.where(rows > cols, fold, jnp.where(rows == cols, line * factor, turned))
    matrix = jnp.concatenate(
        [jnp.concatenate([corner, cross], axis=1), jnp.concatenate([cross.T, last], axis=1)], axis=0
    )
    total = jnp.sum(jnp.sum(matrix * matrix, axis=0, keepdims=True), axis=1, keepdims=True)
    scaling = 2.5 / jnp.sqrt(total)
    coupled = scaling * matrix
    identity = (
        lax.broadcasted_iota(jnp.int32, (order, order), 0) == lax.broadcasted_iota(jnp.int32, (order, order), 1)
    ).astype(jnp.float32)
    row_y, low_z = where_ref[1], where_ref[2]

    def mine(value):
        return jnp.where(low_z == 0, value[:, :half], value[:, half:])

    iterate = None
    for sweep in range(ITERS):
        step_matrix = (5.0 * identity - coupled) * 0.25
        if sweep == 0:
            full[...] = jnp.sqrt(jnp.sqrt(scaling)) * step_matrix
            for chunk in range(16):
                start = pl.multiple_of(32 * chunk + 8 * row_y, 8)
                picked[8 * chunk : 8 * chunk + 8, :] = full[pl.ds(start, 8), :]
            iterate = picked[...]
        else:
            iterate = product(split(iterate), split(step_matrix))
        if sweep < ITERS - 1:
            parts = split(step_matrix)
            squared = split(square(parts))
            fourth = split(square(squared))
            if sweep == ITERS - 2:
                coupled, identity = mine(coupled), mine(identity)
                coupled = product(fourth, split(coupled))
            else:
                coupled = symmetric(fourth, split(coupled))
    for core in range(2):
        out_ref[16 * core : 16 * core + 16] = iterate[:, 128 * core : 128 * core + 128].reshape(16, 8, 128)


def inverse_root(where, slabs, factor):
    return pl.pallas_call(
        functools.partial(root_kernel, factor),
        out_shape=jax.ShapeDtypeStruct((32, 8, 128), jnp.float32),
        in_specs=[pl.BlockSpec(memory_space=pltpu.SMEM), pl.BlockSpec(memory_space=pltpu.VMEM)],
        out_specs=pl.BlockSpec(memory_space=pltpu.VMEM),
        scratch_shapes=[pltpu.VMEM((512, 512), jnp.float32), pltpu.VMEM((128, 512), jnp.float32)],
        compiler_params=pltpu.CompilerParams(vmem_limit_bytes=24 * MIB),
        name="inverse_root",
    )(where, slabs)


def swap(value, name, odd):
    if name in ("x1", "x2", "y1", "y2"):
        flip = 1 if name[1] == "1" else 3
        return lax.ppermute(value, name[0], [(i, i ^ flip) for i in range(4)])
    if not odd:
        return lax.ppermute(value, "z_lo", [(0, 1), (1, 0)])
    pairs = []
    for high in range(4):
        pairs += [(4 + high, (high + 1) % 4), ((high + 1) % 4, 4 + high)]
    return lax.ppermute(value, ("z_lo", "z_hi"), pairs)


def after(value, before):
    return lax.optimization_barrier((value, before))[0]


def body(grads):
    local_grads = grads[0]
    order = local_grads.shape[1]
    where = jnp.stack([lax.axis_index(name).astype(jnp.int32) for name in ("x", "y", "z_lo", "core")])
    factor = 1.0 / (256 * order)
    own, came, keeps, sends = [], [], [], []

    def enter(part):
        blocks = local_grads[4 * part : 4 * part + 4]
        if part:
            blocks = after(local_grads, away_of[-1])[4 * part : 4 * part + 4]
        stays, away = gram(part, where, blocks)
        away_of.append(away)
        own.append(stays)
        came.append(lax.ppermute(away, "core", [(0, 1), (1, 0)]))

    def depart(lane):
        halves = [[], []]
        for part in range(3):
            for which, base, _, size in pieces_of(part):
                if which == lane:
                    other = came[part]
                    for half, first in zip(halves, (base, base + 16 * size)):
                        rows = slice(first, first + 16 * size)
                        half.append((own[part][rows] + other[rows]).reshape(16, size, 128))
        keep, send = (half[0] if len(half) == 1 else jnp.concatenate(half, axis=1) for half in halves)
        keeps.append(keep)
        sends.append(send)

    away_of = []
    enter(0)
    enter(1)
    depart(0)
    enter(2)
    for lane in range(1, len(LANES)):
        depart(lane)
    for step in range(3):
        for lane, (order, odd, _) in enumerate(LANES):
            summed = keeps[lane] + swap(sends[lane], order[step], odd)
            middle = summed.shape[0] // 2
            keeps[lane], sends[lane] = summed[:middle], summed[middle:]
    done = [[], []]
    for (order, _, _), keep, send in zip(LANES, keeps, sends):
        done[order[3] == "x1"].append(jnp.concatenate([keep, send]))
    even, odd = (jnp.concatenate(lanes, axis=1) for lanes in done)
    for along in ("x", "y"):
        middle = even.shape[0] // 2
        even_keep, even_send = lax.optimization_barrier((even[:middle], even[middle:]))
        odd_keep, odd_send = lax.optimization_barrier((odd[:middle], odd[middle:]))
        even_came, odd_came = lax.optimization_barrier(
            (swap(even_send, along + "2", False), swap(odd_send, along + "1", True))
        )
        even, odd = even_keep + even_came, odd_keep + odd_came
    even, odd = even[0], odd[0]
    held = {}
    for total, last in ((even, "x2"), (odd, "x1")):
        first = 0
        for order, _, pieces in LANES:
            if order[3] != last:
                continue
            for piece in pieces:
                held[piece[:2]] = total[first : first + piece[2]]
                first += piece[2]
    parts = [jnp.concatenate([held[key] for key in sorted(held) if key[0] == part]) for part in range(3)]
    parts = jnp.stack(parts + parts[:1])
    high_z = lax.axis_index("z_hi")
    pick = [lax.dynamic_index_in_dim(parts, lax.bitwise_xor(high_z, k), 0, False) for k in range(4)]
    slab = pick[0] + sum(lax.ppermute(pick[k], "z_hi", [(i, i ^ k) for i in range(4)]) for k in (1, 2, 3))
    slabs = lax.all_to_all(
        jnp.broadcast_to(slab[None], (SLABS, UNIT, 128)), ("y", "z_lo"), 0, 0, tiled=True
    )
    pieces = inverse_root(where, slabs, factor)
    arrived = lax.all_to_all(pieces, ("core", "z_hi", "x"), 0, 0, tiled=True)
    return arrived.reshape(2, 16, 8, 128)[:, :12]


def solution(mesh):
    axes = ("z_lo", "core", "z_hi", "x", "y")
    fine = Mesh(mesh.devices.reshape(2, 2, 4, 4, 4), axes)
    return jax.shard_map(
        body,
        mesh=fine,
        in_specs=(P(axes, None, None, None),),
        out_specs=P(None, None, ("z_hi", "x", "y"), ("z_lo", "core")),
        check_vma=False,
    )
```

```python
import functools

import jax
import jax.numpy as jnp
from jax import lax
from jax.experimental import pallas as pl
from jax.experimental.pallas import tpu as pltpu
from jax.sharding import Mesh
from jax.sharding import PartitionSpec as P

ITERS = 4
SLABS = 8
UNIT = 136
LANES = (
    (("x1", "y1", "z", "x2", "y2"), False, ((0, 0, 88),)),
    (("x2", "y2", "z", "x1", "y1"), True, ((0, 88, 48), (1, 0, 32),)),
    (("y1", "z", "x1", "x2", "y2"), False, ((1, 32, 80),)),
    (("y2", "z", "x2", "x1", "y1"), True, ((1, 112, 24), (2, 0, 56),)),
    (("z", "x2", "y2", "x1", "y1"), False, ((2, 56, 80),)),
)
MIB = 1024 * 1024


def pieces_of(part):
    found, base = [], 0
    for lane, (_, _, pieces) in enumerate(LANES):
        for piece in pieces:
            if piece[0] == part:
                found.append((lane, base, piece[1], piece[2]))
                base += 32 * piece[2]
    return found


def place(order, flags):
    at = 0
    for name in order:
        at = at * 2 + flags[name]
    return at


def gram_kernel(part, where_ref, grads_ref, own_ref, away_ref):
    pieces = pieces_of(part)
    col_x, row_y, low_z, core = where_ref[0], where_ref[1], where_ref[2], where_ref[3]
    half = grads_ref.shape[-1] // 2
    slab_rows = half // SLABS
    rows = lax.broadcasted_iota(jnp.int32, (half, half), 0)
    cols = lax.broadcasted_iota(jnp.int32, (half, half), 1)
    upper = rows <= cols
    line_rows = lax.broadcasted_iota(jnp.int32, (slab_rows, 128), 0)
    line_cols = lax.broadcasted_iota(jnp.int32, (slab_rows, 128), 1)
    mult = functools.partial(jnp.dot, preferred_element_type=jnp.float32)
    spots = []
    for slab in range(SLABS):
        from_y = lax.bitwise_xor(row_y, slab // 2)
        high = lax.shift_right_logical(from_y, 1)
        flags = {
            "x1": 0,
            "x2": 0,
            "y1": lax.bitwise_xor(lax.bitwise_and(from_y, 1), high),
            "y2": high,
            "z": lax.bitwise_xor(low_z, slab % 2),
        }
        spots.append([place(LANES[lane][0], flags) for lane, _, _, _ in pieces])

    for step in range(4):
        relative = (step & 1) ^ (3 * (step >> 1))
        block = grads_ref[lax.bitwise_xor(col_x, relative)]
        flipped = block.T
        first = jnp.where(core == 0, block, flipped)
        second = jnp.where(core == 0, flipped, block)
        flags = {"x1": step & 1, "x2": step >> 1, "y1": 0, "y2": 0, "z": 0}
        bases = [base + place(LANES[lane][0], flags) * size for lane, base, _, size in pieces]
        for lhs, rhs, out_ref in ((second, first, away_ref), (first, second, own_ref)):
            corner = mult(lhs[:half], rhs[:, :half])
            right = mult(lhs, rhs[:, half:])
            cross, last = right[:half], right[half:]
            fold = jnp.where(upper, corner, last)
            for slab in range(SLABS):
                mine = slice(slab * slab_rows, (slab + 1) * slab_rows)
                near = slab * slab_rows // 128 * 128
                square = last[mine, near : near + 128]
                line = jnp.sum(
                    jnp.where(line_cols - line_rows == slab * slab_rows - near, square, 0.0), axis=0, keepdims=True
                )
                content = (
                    cross[mine, :128],
                    cross[mine, 128:],
                    fold[mine, :128],
                    fold[mine, 128:],
                    jnp.broadcast_to(line, (8, 128)),
                )
                for spot, base, (_, _, first_row, size) in zip(spots[slab], bases, pieces):
                    start = pl.multiple_of(spot * size + base, 8)
                    for band, value in enumerate(content):
                        low = max(band * slab_rows, first_row)
                        top = min(band * slab_rows + value.shape[0], first_row + size)
                        if low < top:
                            cut = value[low - band * slab_rows : top - band * slab_rows]
                            out_ref[pl.ds(start + low - first_row, top - low), :] = cut


def gram(part, where, grads):
    shape = jax.ShapeDtypeStruct((32 * UNIT, 128), jnp.float32)
    whole = pl.BlockSpec(memory_space=pltpu.VMEM)
    return pl.pallas_call(
        functools.partial(gram_kernel, part),
        out_shape=(shape, shape),
        in_specs=[pl.BlockSpec(memory_space=pltpu.SMEM), whole],
        out_specs=(whole, whole),
        compiler_params=pltpu.CompilerParams(vmem_limit_bytes=16 * MIB),
        name=f"gram_{part}",
    )(where, grads)


def split(value):
    high = value.astype(jnp.bfloat16)
    return high, (value - high.astype(jnp.float32)).astype(jnp.bfloat16)


def product(left, right):
    mult = functools.partial(jnp.dot, preferred_element_type=jnp.float32)
    return mult(left[0], right[0]) + (mult(left[0], right[1]) + mult(left[1], right[0]))


def symmetric(left, right):
    top = product([half[:256] for half in left], right)
    last = product([half[256:] for half in left], [half[:, 256:] for half in right])
    return jnp.concatenate([top, jnp.concatenate([top[:, 256:].T, last], axis=1)], axis=0)


def square(parts):
    mult = functools.partial(jnp.dot, preferred_element_type=jnp.float32)
    high, low = parts
    mixed = mult(high, low)
    top = mult(high[:256], high)
    last = mult(high[256:], high[:, 256:])
    first = top[:, :256] + (mixed[:256, :256] + mixed[:256, :256].T)
    cross = top[:, 256:] + (mixed[:256, 256:] + mixed[256:, :256].T)
    last = last + (mixed[256:, 256:] + mixed[256:, 256:].T)
    return jnp.concatenate(
        [jnp.concatenate([first, cross], axis=1), jnp.concatenate([cross.T, last], axis=1)], axis=0
    )


def root_kernel(factor, where_ref, slabs_ref, out_ref, full, picked):
    half = 256
    order = 2 * half
    slab_rows = half // SLABS
    rows = lax.broadcasted_iota(jnp.int32, (half, half), 0)
    cols = lax.broadcasted_iota(jnp.int32, (half, half), 1)

    def gathered(first):
        left = jnp.concatenate([slabs_ref[s, first : first + slab_rows] for s in range(SLABS)], axis=0)
        right = jnp.concatenate(
            [slabs_ref[s, first + slab_rows : first + 2 * slab_rows] for s in range(SLABS)], axis=0
        )
        return jnp.concatenate([left, right], axis=1) * factor

    cross = gathered(0)
    fold = gathered(64)
    line = jnp.concatenate(
        [sum(slabs_ref[s, 128:129] for s in group) for group in (range(4), range(4, 8))], axis=1
    )
    turned = fold.T
    corner = jnp.where(rows <= cols, fold, turned)
    last = jnp.where(rows > cols, fold, jnp.where(rows == cols, line * factor, turned))
    matrix = jnp.concatenate(
        [jnp.concatenate([corner, cross], axis=1), jnp.concatenate([cross.T, last], axis=1)], axis=0
    )
    total = jnp.sum(jnp.sum(matrix * matrix, axis=0, keepdims=True), axis=1, keepdims=True)
    scaling = 2.5 / jnp.sqrt(total)
    coupled = scaling * matrix
    identity = (
        lax.broadcasted_iota(jnp.int32, (order, order), 0) == lax.broadcasted_iota(jnp.int32, (order, order), 1)
    ).astype(jnp.float32)
    row_y, low_z = where_ref[1], where_ref[2]

    def mine(value):
        return jnp.where(low_z == 0, value[:, :half], value[:, half:])

    iterate = None
    for sweep in range(ITERS):
        step_matrix = (5.0 * identity - coupled) * 0.25
        if sweep == 0:
            full[...] = jnp.sqrt(jnp.sqrt(scaling)) * step_matrix
            for chunk in range(16):
                start = pl.multiple_of(32 * chunk + 8 * row_y, 8)
                picked[8 * chunk : 8 * chunk + 8, :] = full[pl.ds(start, 8), :]
            iterate = picked[...]
        else:
            iterate = product(split(iterate), split(step_matrix))
        if sweep < ITERS - 1:
            parts = split(step_matrix)
            squared = split(square(parts))
            fourth = split(square(squared))
            if sweep == ITERS - 2:
                coupled, identity = mine(coupled), mine(identity)
                coupled = product(fourth, split(coupled))
            else:
                coupled = symmetric(fourth, split(coupled))
    for core in range(2):
        out_ref[16 * core : 16 * core + 16] = iterate[:, 128 * core : 128 * core + 128].reshape(16, 8, 128)


def inverse_root(where, slabs, factor):
    return pl.pallas_call(
        functools.partial(root_kernel, factor),
        out_shape=jax.ShapeDtypeStruct((32, 8, 128), jnp.float32),
        in_specs=[pl.BlockSpec(memory_space=pltpu.SMEM), pl.BlockSpec(memory_space=pltpu.VMEM)],
        out_specs=pl.BlockSpec(memory_space=pltpu.VMEM),
        scratch_shapes=[pltpu.VMEM((512, 512), jnp.float32), pltpu.VMEM((128, 512), jnp.float32)],
        compiler_params=pltpu.CompilerParams(vmem_limit_bytes=24 * MIB),
        name="inverse_root",
    )(where, slabs)


def swap(value, name, odd):
    if name in ("x1", "x2", "y1", "y2"):
        flip = 1 if name[1] == "1" else 3
        return lax.ppermute(value, name[0], [(i, i ^ flip) for i in range(4)])
    if not odd:
        return lax.ppermute(value, "z_lo", [(0, 1), (1, 0)])
    pairs = []
    for high in range(4):
        pairs += [(4 + high, (high + 1) % 4), ((high + 1) % 4, 4 + high)]
    return lax.ppermute(value, ("z_lo", "z_hi"), pairs)


def after(value, before):
    return lax.optimization_barrier((value, before))[0]


def body(grads):
    local_grads = grads[0]
    order = local_grads.shape[1]
    where = jnp.stack([lax.axis_index(name).astype(jnp.int32) for name in ("x", "y", "z_lo", "core")])
    factor = 1.0 / (256 * order)
    own, came, keeps, sends = [], [], [], []

    def enter(part):
        blocks = local_grads[4 * part : 4 * part + 4]
        if part:
            blocks = after(local_grads, away_of[-1])[4 * part : 4 * part + 4]
        stays, away = gram(part, where, blocks)
        away_of.append(away)
        own.append(stays)
        came.append(lax.ppermute(away, "core", [(0, 1), (1, 0)]))

    def depart(lane):
        halves = [[], []]
        for part in range(3):
            for which, base, _, size in pieces_of(part):
                if which == lane:
                    other = came[part]
                    for half, first in zip(halves, (base, base + 16 * size)):
                        rows = slice(first, first + 16 * size)
                        half.append((own[part][rows] + other[rows]).reshape(16, size, 128))
        keep, send = (half[0] if len(half) == 1 else jnp.concatenate(half, axis=1) for half in halves)
        keeps.append(keep)
        sends.append(send)

    away_of = []
    enter(0)
    enter(1)
    depart(0)
    enter(2)
    for lane in range(1, len(LANES)):
        depart(lane)
    for step in range(3):
        for lane, (order, odd, _) in enumerate(LANES):
            summed = keeps[lane] + swap(sends[lane], order[step], odd)
            middle = summed.shape[0] // 2
            keeps[lane], sends[lane] = summed[:middle], summed[middle:]
    done = [[], []]
    for (order, _, _), keep, send in zip(LANES, keeps, sends):
        done[order[3] == "x1"].append(jnp.concatenate([keep, send]))
    even, odd = (jnp.concatenate(lanes, axis=1) for lanes in done)
    for along in ("x", "y"):
        middle = even.shape[0] // 2
        even_keep, even_send = lax.optimization_barrier((even[:middle], even[middle:]))
        odd_keep, odd_send = lax.optimization_barrier((odd[:middle], odd[middle:]))
        even_came, odd_came = swap(even_send, along + "2", False), swap(odd_send, along + "1", True)
        if along == "y":
            even_came, odd_came = lax.optimization_barrier((even_came, odd_came))
        even, odd = even_keep + even_came, odd_keep + odd_came
    even, odd = even[0], odd[0]
    held = {}
    for total, last in ((even, "x2"), (odd, "x1")):
        first = 0
        for order, _, pieces in LANES:
            if order[3] != last:
                continue
            for piece in pieces:
                held[piece[:2]] = total[first : first + piece[2]]
                first += piece[2]
    parts = [jnp.concatenate([held[key] for key in sorted(held) if key[0] == part]) for part in range(3)]
    parts = jnp.stack(parts + parts[:1])
    high_z = lax.axis_index("z_hi")
    pick = [lax.dynamic_index_in_dim(parts, lax.bitwise_xor(high_z, k), 0, False) for k in range(4)]
    slab = pick[0] + sum(lax.ppermute(pick[k], "z_hi", [(i, i ^ k) for i in range(4)]) for k in (1, 2, 3))
    slabs = lax.all_to_all(
        jnp.broadcast_to(slab[None], (SLABS, UNIT, 128)), ("y", "z_lo"), 0, 0, tiled=True
    )
    pieces = inverse_root(where, slabs, factor)
    arrived = lax.all_to_all(pieces, ("core", "z_hi", "x"), 0, 0, tiled=True)
    return arrived.reshape(2, 16, 8, 128)[:, :12]


def solution(mesh):
    axes = ("z_lo", "core", "z_hi", "x", "y")
    fine = Mesh(mesh.devices.reshape(2, 2, 4, 4, 4), axes)
    return jax.shard_map(
        body,
        mesh=fine,
        in_specs=(P(axes, None, None, None),),
        out_specs=P(None, None, ("z_hi", "x", "y"), ("z_lo", "core")),
        check_vma=False,
    )
```

```python
import functools

import jax
import jax.numpy as jnp
from jax import lax
from jax.experimental import pallas as pl
from jax.experimental.pallas import tpu as pltpu
from jax.sharding import Mesh
from jax.sharding import PartitionSpec as P

ITERS = 4
SLABS = 8
UNIT = 136
LANES = (
    (("x1", "y1", "z", "x2", "y2"), False, ((0, 0, 88),)),
    (("x2", "y2", "z", "x1", "y1"), True, ((0, 88, 48), (1, 0, 32),)),
    (("y1", "z", "x1", "x2", "y2"), False, ((1, 32, 80),)),
    (("y2", "z", "x2", "x1", "y1"), True, ((1, 112, 24), (2, 0, 56),)),
    (("z", "x2", "y2", "x1", "y1"), False, ((2, 56, 80),)),
)
MIB = 1024 * 1024


def pieces_of(part):
    found, base = [], 0
    for lane, (_, _, pieces) in enumerate(LANES):
        for piece in pieces:
            if piece[0] == part:
                found.append((lane, base, piece[1], piece[2]))
                base += 32 * piece[2]
    return found


def place(order, flags):
    at = 0
    for name in order:
        at = at * 2 + flags[name]
    return at


def gram_kernel(part, where_ref, grads_ref, own_ref, away_ref):
    pieces = pieces_of(part)
    col_x, row_y, low_z, core = where_ref[0], where_ref[1], where_ref[2], where_ref[3]
    half = grads_ref.shape[-1] // 2
    slab_rows = half // SLABS
    rows = lax.broadcasted_iota(jnp.int32, (half, half), 0)
    cols = lax.broadcasted_iota(jnp.int32, (half, half), 1)
    upper = rows <= cols
    line_rows = lax.broadcasted_iota(jnp.int32, (slab_rows, 128), 0)
    line_cols = lax.broadcasted_iota(jnp.int32, (slab_rows, 128), 1)
    mult = functools.partial(jnp.dot, preferred_element_type=jnp.float32)
    spots = []
    for slab in range(SLABS):
        from_y = lax.bitwise_xor(row_y, slab // 2)
        high = lax.shift_right_logical(from_y, 1)
        flags = {
            "x1": 0,
            "x2": 0,
            "y1": lax.bitwise_xor(lax.bitwise_and(from_y, 1), high),
            "y2": high,
            "z": lax.bitwise_xor(low_z, slab % 2),
        }
        spots.append([place(LANES[lane][0], flags) for lane, _, _, _ in pieces])

    for step in range(4):
        relative = (step & 1) ^ (3 * (step >> 1))
        block = grads_ref[lax.bitwise_xor(col_x, relative)]
        flipped = block.T
        first = jnp.where(core == 0, block, flipped)
        second = jnp.where(core == 0, flipped, block)
        flags = {"x1": step & 1, "x2": step >> 1, "y1": 0, "y2": 0, "z": 0}
        bases = [base + place(LANES[lane][0], flags) * size for lane, base, _, size in pieces]
        for lhs, rhs, out_ref in ((second, first, away_ref), (first, second, own_ref)):
            corner = mult(lhs[:half], rhs[:, :half])
            right = mult(lhs, rhs[:, half:])
            cross, last = right[:half], right[half:]
            fold = jnp.where(upper, corner, last)
            for slab in range(SLABS):
                mine = slice(slab * slab_rows, (slab + 1) * slab_rows)
                near = slab * slab_rows // 128 * 128
                square = last[mine, near : near + 128]
                line = jnp.sum(
                    jnp.where(line_cols - line_rows == slab * slab_rows - near, square, 0.0), axis=0, keepdims=True
                )
                content = (
                    cross[mine, :128],
                    cross[mine, 128:],
                    fold[mine, :128],
                    fold[mine, 128:],
                    jnp.broadcast_to(line, (8, 128)),
                )
                for spot, base, (_, _, first_row, size) in zip(spots[slab], bases, pieces):
                    start = pl.multiple_of(spot * size + base, 8)
                    for band, value in enumerate(content):
                        low = max(band * slab_rows, first_row)
                        top = min(band * slab_rows + value.shape[0], first_row + size)
                        if low < top:
                            cut = value[low - band * slab_rows : top - band * slab_rows]
                            out_ref[pl.ds(start + low - first_row, top - low), :] = cut


def gram(part, where, grads):
    shape = jax.ShapeDtypeStruct((32 * UNIT, 128), jnp.float32)
    whole = pl.BlockSpec(memory_space=pltpu.VMEM)
    return pl.pallas_call(
        functools.partial(gram_kernel, part),
        out_shape=(shape, shape),
        in_specs=[pl.BlockSpec(memory_space=pltpu.SMEM), whole],
        out_specs=(whole, whole),
        compiler_params=pltpu.CompilerParams(vmem_limit_bytes=16 * MIB),
        name=f"gram_{part}",
    )(where, grads)


def split(value):
    high = value.astype(jnp.bfloat16)
    return high, (value - high.astype(jnp.float32)).astype(jnp.bfloat16)


def product(left, right):
    mult = functools.partial(jnp.dot, preferred_element_type=jnp.float32)
    return mult(left[0], right[0]) + (mult(left[0], right[1]) + mult(left[1], right[0]))


def symmetric(left, right):
    top = product([half[:256] for half in left], right)
    last = product([half[256:] for half in left], [half[:, 256:] for half in right])
    return jnp.concatenate([top, jnp.concatenate([top[:, 256:].T, last], axis=1)], axis=0)


def square(parts, rows=None):
    mult = functools.partial(jnp.dot, preferred_element_type=jnp.float32)
    high, low = parts
    moved = None
    if rows is None:
        mixed = mult(high, low)
        top = mult(high[:256], high)
    else:
        count = rows[0].shape[0]
        mixed = mult(jnp.concatenate([high, rows[0]], axis=0), low)
        top = mult(jnp.concatenate([high[:256], *rows], axis=0), high)
        moved = top[256 : 256 + count] + (mixed[512:] + top[256 + count :])
        top, mixed = top[:256], mixed[:512]
    last = mult(high[256:], high[:, 256:])
    first = top[:, :256] + (mixed[:256, :256] + mixed[:256, :256].T)
    cross = top[:, 256:] + (mixed[:256, 256:] + mixed[256:, :256].T)
    last = last + (mixed[256:, 256:] + mixed[256:, 256:].T)
    whole = jnp.concatenate(
        [jnp.concatenate([first, cross], axis=1), jnp.concatenate([cross.T, last], axis=1)], axis=0
    )
    return whole, moved


def root_kernel(factor, where_ref, slabs_ref, out_ref, full, picked):
    half = 256
    order = 2 * half
    slab_rows = half // SLABS
    rows = lax.broadcasted_iota(jnp.int32, (half, half), 0)
    cols = lax.broadcasted_iota(jnp.int32, (half, half), 1)

    def gathered(first):
        left = jnp.concatenate([slabs_ref[s, first : first + slab_rows] for s in range(SLABS)], axis=0)
        right = jnp.concatenate(
            [slabs_ref[s, first + slab_rows : first + 2 * slab_rows] for s in range(SLABS)], axis=0
        )
        return jnp.concatenate([left, right], axis=1) * factor

    cross = gathered(0)
    fold = gathered(64)
    line = jnp.concatenate(
        [sum(slabs_ref[s, 128:129] for s in group) for group in (range(4), range(4, 8))], axis=1
    )
    turned = fold.T
    corner = jnp.where(rows <= cols, fold, turned)
    last = jnp.where(rows > cols, fold, jnp.where(rows == cols, line * factor, turned))
    matrix = jnp.concatenate(
        [jnp.concatenate([corner, cross], axis=1), jnp.concatenate([cross.T, last], axis=1)], axis=0
    )
    total = jnp.sum(jnp.sum(matrix * matrix, axis=0, keepdims=True), axis=1, keepdims=True)
    scaling = 2.5 / jnp.sqrt(total)
    coupled = scaling * matrix
    identity = (
        lax.broadcasted_iota(jnp.int32, (order, order), 0) == lax.broadcasted_iota(jnp.int32, (order, order), 1)
    ).astype(jnp.float32)
    row_y, low_z = where_ref[1], where_ref[2]

    def mine(value):
        return jnp.where(low_z == 0, value[:, :half], value[:, half:])

    iterate = None
    for sweep in range(ITERS):
        step_matrix = (5.0 * identity - coupled) * 0.25
        if sweep == 0:
            full[...] = jnp.sqrt(jnp.sqrt(scaling)) * step_matrix
            for chunk in range(16):
                start = pl.multiple_of(32 * chunk + 8 * row_y, 8)
                picked[8 * chunk : 8 * chunk + 8, :] = full[pl.ds(start, 8), :]
            iterate = picked[...]
        elif sweep == ITERS - 1:
            iterate = product(split(iterate), split(step_matrix))
        if sweep < ITERS - 1:
            squared, moved = square(split(step_matrix), split(iterate) if sweep else None)
            iterate = moved if sweep else iterate
            squared = split(squared)
            fourth = split(square(squared)[0])
            if sweep == ITERS - 2:
                coupled, identity = mine(coupled), mine(identity)
                coupled = product(fourth, split(coupled))
            else:
                coupled = symmetric(fourth, split(coupled))
    for core in range(2):
        out_ref[16 * core : 16 * core + 16] = iterate[:, 128 * core : 128 * core + 128].reshape(16, 8, 128)


def inverse_root(where, slabs, factor):
    return pl.pallas_call(
        functools.partial(root_kernel, factor),
        out_shape=jax.ShapeDtypeStruct((32, 8, 128), jnp.float32),
        in_specs=[pl.BlockSpec(memory_space=pltpu.SMEM), pl.BlockSpec(memory_space=pltpu.VMEM)],
        out_specs=pl.BlockSpec(memory_space=pltpu.VMEM),
        scratch_shapes=[pltpu.VMEM((512, 512), jnp.float32), pltpu.VMEM((128, 512), jnp.float32)],
        compiler_params=pltpu.CompilerParams(vmem_limit_bytes=24 * MIB),
        name="inverse_root",
    )(where, slabs)


def swap(value, name, odd):
    if name in ("x1", "x2", "y1", "y2"):
        flip = 1 if name[1] == "1" else 3
        return lax.ppermute(value, name[0], [(i, i ^ flip) for i in range(4)])
    if not odd:
        return lax.ppermute(value, "z_lo", [(0, 1), (1, 0)])
    pairs = []
    for high in range(4):
        pairs += [(4 + high, (high + 1) % 4), ((high + 1) % 4, 4 + high)]
    return lax.ppermute(value, ("z_lo", "z_hi"), pairs)


def after(value, before):
    return lax.optimization_barrier((value, before))[0]


def body(grads):
    local_grads = grads[0]
    order = local_grads.shape[1]
    where = jnp.stack([lax.axis_index(name).astype(jnp.int32) for name in ("x", "y", "z_lo", "core")])
    factor = 1.0 / (256 * order)
    own, came, keeps, sends = [], [], [], []

    def enter(part):
        blocks = local_grads[4 * part : 4 * part + 4]
        if part:
            blocks = after(local_grads, away_of[-1])[4 * part : 4 * part + 4]
        stays, away = gram(part, where, blocks)
        away_of.append(away)
        own.append(stays)
        came.append(lax.ppermute(away, "core", [(0, 1), (1, 0)]))

    def depart(lane):
        halves = [[], []]
        for part in range(3):
            for which, base, _, size in pieces_of(part):
                if which == lane:
                    other = came[part]
                    for half, first in zip(halves, (base, base + 16 * size)):
                        rows = slice(first, first + 16 * size)
                        half.append((own[part][rows] + other[rows]).reshape(16, size, 128))
        keep, send = (half[0] if len(half) == 1 else jnp.concatenate(half, axis=1) for half in halves)
        keeps.append(keep)
        sends.append(send)

    away_of = []
    enter(0)
    enter(1)
    depart(0)
    enter(2)
    for lane in range(1, len(LANES)):
        depart(lane)
    for step in range(3):
        for lane, (order, odd, _) in enumerate(LANES):
            summed = keeps[lane] + swap(sends[lane], order[step], odd)
            middle = summed.shape[0] // 2
            keeps[lane], sends[lane] = summed[:middle], summed[middle:]
    done = [[], []]
    for (order, _, _), keep, send in zip(LANES, keeps, sends):
        done[order[3] == "x1"].append(jnp.concatenate([keep, send]))
    even, odd = (jnp.concatenate(lanes, axis=1) for lanes in done)
    for along in ("x", "y"):
        middle = even.shape[0] // 2
        even_keep, even_send = lax.optimization_barrier((even[:middle], even[middle:]))
        odd_keep, odd_send = lax.optimization_barrier((odd[:middle], odd[middle:]))
        even_came, odd_came = lax.optimization_barrier(
            (swap(even_send, along + "2", False), swap(odd_send, along + "1", True))
        )
        even, odd = even_keep + even_came, odd_keep + odd_came
    even, odd = even[0], odd[0]
    held = {}
    for total, last in ((even, "x2"), (odd, "x1")):
        first = 0
        for order, _, pieces in LANES:
            if order[3] != last:
                continue
            for piece in pieces:
                held[piece[:2]] = total[first : first + piece[2]]
                first += piece[2]
    parts = [jnp.concatenate([held[key] for key in sorted(held) if key[0] == part]) for part in range(3)]
    parts = jnp.stack(parts + parts[:1])
    high_z = lax.axis_index("z_hi")
    pick = [lax.dynamic_index_in_dim(parts, lax.bitwise_xor(high_z, k), 0, False) for k in range(4)]
    slab = pick[0] + sum(lax.ppermute(pick[k], "z_hi", [(i, i ^ k) for i in range(4)]) for k in (1, 2, 3))
    slabs = lax.all_to_all(
        jnp.broadcast_to(slab[None], (SLABS, UNIT, 128)), ("y", "z_lo"), 0, 0, tiled=True
    )
    pieces = inverse_root(where, slabs, factor)
    arrived = lax.all_to_all(pieces, ("core", "z_hi", "x"), 0, 0, tiled=True)
    return arrived.reshape(2, 16, 8, 128)[:, :12]


def solution(mesh):
    axes = ("z_lo", "core", "z_hi", "x", "y")
    fine = Mesh(mesh.devices.reshape(2, 2, 4, 4, 4), axes)
    return jax.shard_map(
        body,
        mesh=fine,
        in_specs=(P(axes, None, None, None),),
        out_specs=P(None, None, ("z_hi", "x", "y"), ("z_lo", "core")),
        check_vma=False,
    )
```
